256 devices in a mesh: seq: 32 (over z_hi, y, core), head: 8 (over z_lo, x).
Axes of the slice: x: 4, y: 4, z: 8 (z_hi: 4, z_lo: 2; z = z_hi * 2 + z_lo), core: 2. Of those that a mesh axis runs over, the one named last changes fastest.
Arguments:
- queries: bfloat16 [384, 64, 128], P('seq', 'head'), may hold values from -88 to 88
- prompt_keys: bfloat16 [65536, 8, 128], P('seq', 'head'), may hold values from -4 to 4
- prompt_values: bfloat16 [65536, 8, 128], P('seq', 'head'), may hold values from -6 to 6
- suffix_keys: bfloat16 [384, 8, 1024, 128], P('seq', 'head'), may hold values from -8 to 8
- suffix_values: bfloat16 [384, 8, 1024, 128], P('seq', 'head'), may hold values from -6 to 6
- suffix_lengths: int32 [384], P('seq'), may hold values from 1 to 1024, as said below
- slot_of_sample: int32 [384], replicated, may hold values from 0 to 383, each once
- out_weight: bfloat16 [8192, 5120], P('head', 'seq'), may hold values from -0.0625 to 0.0625
Outputs:
- projected: float32 [384, 5120], P('head', 'seq')
The draws below stay inside these ranges and needn't reach their ends.
Inputs may be any that keep to these rules, and one draw needn't show every extreme that they name: `suffix_lengths`: slot j is held with the samples of seq index j // 12; some slot has exactly 1024 live tokens. `slot_of_sample`: each slot is named once.
All inputs are finite; a program needn't handle non-finite values.
Results may differ from the reference program's by a relative error of at most 0.006.
Values may be sent and summed in bfloat16 or wider, within the bound.
No kernel may reach another device: no remote copies, remote signals or barrier semaphores. Data moves between devices by JAX's collectives and lax.ppermute only.
A program may use at most 64 MiB of HBM per device.

```python
import math
import jax
import jax.numpy as jnp
from jax import lax

HEADS = 64
KV_HEADS = 8
HEAD_DIM = 128
D = 5120
SUFFIX = 1024
PROMPT = 65536
SAMPLES = 384


def draw_queries(key, part):
    key = jax.random.fold_in(key, 1)
    base = jnp.clip(3.0 * jax.random.normal(key, (SAMPLES, HEADS, HEAD_DIM), jnp.float32), -12.0, 12.0)
    return base.astype(jnp.bfloat16)


def draw_prompt_keys(key, part):
    key = jax.random.fold_in(key, 2)
    base = jnp.clip(jax.random.normal(key, (PROMPT, KV_HEADS, HEAD_DIM), jnp.float32), -4.0, 4.0)
    return base.astype(jnp.bfloat16)


def draw_suffix_lengths(key, part):
    key = jax.random.fold_in(key, 3)
    first_key, second_key = jax.random.split(key)
    lengths = jax.random.randint(first_key, (SAMPLES,), 1, SUFFIX + 1, jnp.int32)
    picked = jax.random.randint(second_key, (), 0, SAMPLES, jnp.int32)
    return lengths.at[picked].set(SUFFIX)


def levels(stream_key, dims, pieces, least, high):
    level, own = 1.0, jax.random.fold_in(stream_key, 6)
    for dim, shards_of in pieces:
        steps = jnp.exp(jax.random.uniform(jax.random.fold_in(own, dim), (shards_of,), jnp.float32, least / len(pieces), high / len(pieces)))
        level = level * jnp.repeat(steps, dims[dim] // shards_of).reshape([-1 if axis == dim else 1 for axis in range(len(dims))])
    return level


def centred(key, extent, spread, reach, cuts=(), dtype=jnp.bfloat16):
    drawn = spread * jax.random.normal(key, extent, jnp.float32)
    if cuts:
        drawn = drawn * levels(key, extent, cuts, -0.22, 0.18)
    return jnp.clip(drawn, -reach, reach).astype(dtype)


def setup_inputs(seed: int = 0) -> dict:
    streams_of = jax.random.split(jax.random.key(seed), 9)
    return {
        "queries": draw_queries(jax.random.fold_in(streams_of[8], 71), 0),
        "prompt_keys": draw_prompt_keys(jax.random.fold_in(streams_of[8], 71), 0),
        "prompt_values": centred(streams_of[2], (PROMPT, KV_HEADS, HEAD_DIM), 1.0, 6.0, ((0, 32), (1, 8))),
        "suffix_keys": centred(streams_of[3], (SAMPLES, KV_HEADS, SUFFIX, HEAD_DIM), 1.4, 8.0, ((0, 32), (1, 8))),
        "suffix_values": centred(streams_of[4], (SAMPLES, KV_HEADS, SUFFIX, HEAD_DIM), 1.0, 6.0, ((0, 32), (1, 8))),
        "suffix_lengths": draw_suffix_lengths(jax.random.fold_in(streams_of[8], 71), 0),
        "slot_of_sample": jax.random.permutation(streams_of[6], SAMPLES).astype(jnp.int32),
        "out_weight": centred(streams_of[7], (HEADS * HEAD_DIM, D), (HEADS * HEAD_DIM) ** -0.5, 0.0625, ((0, 8), (1, 32))),
    }


def reference(queries, prompt_keys, prompt_values, suffix_keys, suffix_values, suffix_lengths, slot_of_sample, out_weight):
    total_rows = queries.shape[0]
    block_rows = math.gcd(total_rows, 8)
    group_size = HEADS // KV_HEADS
    score_scale = 1.0 / math.sqrt(HEAD_DIM)
    keys_full = prompt_keys.astype(jnp.float32)
    values_full = prompt_values.astype(jnp.float32)
    prompt_count = prompt_keys.shape[0]

    def one_block(start_row):
        first = start_row.astype(jnp.int32)
        query_block = lax.dynamic_slice_in_dim(queries, first, block_rows, 0).astype(jnp.float32)
        query_block = query_block.reshape(block_rows, KV_HEADS, group_size, HEAD_DIM)
        slots = lax.dynamic_slice_in_dim(slot_of_sample, first, block_rows, 0).astype(jnp.int32)
        tail_keys = suffix_keys[slots].astype(jnp.float32)
        tail_values = suffix_values[slots].astype(jnp.float32)
        lengths = suffix_lengths[slots]
        head_scores = jnp.einsum('bkgd,pkd->bkgp', query_block, keys_full) * score_scale
        tail_scores = jnp.einsum('bkgd,bksd->bkgs', query_block, tail_keys) * score_scale
        positions = jnp.arange(SUFFIX).astype(jnp.int32)
        live_mask = positions[None, None, None, :] < lengths.astype(jnp.int32)[:, None, None, None]
        tail_scores = jnp.where(live_mask, tail_scores, jnp.float32(-1e+30))
        scores = jnp.concatenate([head_scores, tail_scores], axis=-1)
        row_max = lax.optimization_barrier(jnp.max(scores, axis=-1, keepdims=True))
        weights = jnp.exp(scores - row_max)
        row_total = lax.optimization_barrier(jnp.sum(weights, axis=-1))
        rounded = lax.optimization_barrier(weights.astype(jnp.bfloat16)).astype(jnp.float32)
        output = jnp.einsum('bkgp,pkd->bkgd', rounded[..., :prompt_count], values_full)
        output = output + jnp.einsum('bkgs,bksd->bkgd', rounded[..., prompt_count:], tail_values)
        attention = (output / row_total[..., None]).astype(jnp.bfloat16)
        return attention.reshape(block_rows, HEADS * HEAD_DIM)
    starts = jnp.arange(0, total_rows, block_rows).astype(jnp.int32)
    attention = lax.map(one_block, starts).reshape(total_rows, HEADS * HEAD_DIM)
    return jnp.dot(attention, out_weight, preferred_element_type=jnp.float32)
```

```python
import functools
import math

import jax
import jax.numpy as jnp
from jax import lax
from jax.experimental import pallas as pl
from jax.experimental.pallas import tpu as pltpu
from jax.sharding import PartitionSpec as P

Z, Y, C = 4, 4, 2
SEQ = Z * Y * C
HEADS_LOCAL = 8
WIDTH = 128
LOCAL = 12
ROWS = LOCAL * HEADS_LOCAL
CHUNK = Z * ROWS
STATS = 16
PART = CHUNK + STATS
TILES = CHUNK // 128
SUFFIX = 1024
BLOCK = 256
EXPONENT = math.log2(math.e) / math.sqrt(WIDTH)
DEAD = -1e30


def exchange(x, dz, dy, dc):
    def index(z, y, c):
        return (z * Y + y) * C + c

    pairs = [
        (index(z, y, c), index(z ^ dz, y ^ dy, c ^ dc))
        for z in range(Z)
        for y in range(Y)
        for c in range(C)
    ]
    return lax.ppermute(x, "seq", pairs)


def near(x):
    return x.astype(jnp.bfloat16).astype(jnp.float32)


def attention_kernel(
    samples_ref,
    lengths_ref,
    queries_ref,
    keys_ref,
    values_ref,
    tail_keys_ref,
    tail_values_ref,
    first_ref,
    second_ref,
    tail_k,
    tail_v,
    wide,
    scores,
    acc,
    total,
    top,
    sem,
):
    copies = [
        pltpu.make_async_copy(tail_keys_ref, tail_k, sem.at[0]),
        pltpu.make_async_copy(tail_values_ref, tail_v, sem.at[1]),
    ]
    for copy in copies:
        copy.start()
    wide[:, :WIDTH] = values_ref[...]
    wide[:, WIDTH:] = jnp.ones_like(wide[:, WIDTH:])
    nt = (((1,), (1,)), ((), ()))

    def score(block, slot):
        q = queries_ref[pl.ds(block * BLOCK, BLOCK), :]
        scores[slot] = lax.dot_general(q, keys_ref[...], nt, preferred_element_type=jnp.float32)

    def weigh(block, slot):
        s = scores[slot]
        c = near(jnp.max(s, axis=1, keepdims=True) * EXPONENT)
        w = jnp.exp2(s * EXPONENT - c).astype(jnp.bfloat16)
        o = jnp.dot(w, wide[...], preferred_element_type=jnp.float32)
        rows = pl.ds(block * BLOCK, BLOCK)
        acc[rows, :] = o[:, :WIDTH]
        total[rows, :] = o[:, WIDTH:]
        top[rows, :] = jnp.broadcast_to(c, (BLOCK, WIDTH))

    blocks = SEQ * ROWS // BLOCK
    score(0, 0)

    def body(i, carry):
        score(2 * i + 1, 1)
        weigh(2 * i, 0)
        score(jnp.minimum(2 * i + 2, blocks - 1), 0)
        weigh(2 * i + 1, 1)
        return carry

    lax.fori_loop(0, blocks // 2, body, 0)

    for copy in copies:
        copy.wait()
    position = lax.broadcasted_iota(jnp.int32, (HEADS_LOCAL, SUFFIX), 1)
    tails = []
    for j in range(LOCAL):
        row = samples_ref[j]
        base = pl.multiple_of(row // 16 * 16, 16)
        pair = queries_ref[pl.ds(base, 16), :].astype(jnp.float32)
        q = jnp.where(row % 16 == 8, pair[8:], pair[:8]).astype(jnp.bfloat16)
        s = lax.dot_general(q, tail_k[j], nt, preferred_element_type=jnp.float32)
        tails.append(jnp.where(position < lengths_ref[j], s * EXPONENT, DEAD))
    for j in range(LOCAL):
        c = near(jnp.max(tails[j], axis=1, keepdims=True))
        w = jnp.exp2(tails[j] - c)
        t = jnp.sum(w, axis=1, keepdims=True)
        o = jnp.dot(w.astype(jnp.bfloat16), tail_v[j], preferred_element_type=jnp.float32)
        rows = pl.ds(pl.multiple_of(samples_ref[j], 8), 8)
        old = top[rows, :]
        new = jnp.maximum(old, c)
        f, g = jnp.exp2(old - new), jnp.exp2(c - new)
        acc[rows, :] = acc[rows, :] * f + o * g
        total[rows, :] = total[rows, :] * f + t * g
        top[rows, :] = new

    lane = lax.broadcasted_iota(jnp.int32, (128, 128), 1)
    for chunk in range(C * Y):
        part = (first_ref if chunk < Y else second_ref).at[chunk % Y]
        stats = []
        for tile in range(TILES):
            rows = pl.ds(chunk * CHUNK + tile * 128, 128)
            part[pl.ds(tile * 128, 128), :] = acc[rows, :].astype(jnp.bfloat16)
            sums = total[rows, :]
            high = near(sums)
            mixed = jnp.where(lane == 0, top[rows, :], jnp.where(lane == 1, high, sums - high))
            stats.append(jnp.transpose(mixed)[:4])
        stats.append(jnp.zeros((STATS - 4 * TILES, 128), jnp.float32))
        part[pl.ds(CHUNK, STATS), :] = jnp.concatenate(stats, axis=0).astype(jnp.bfloat16)


def merge_tile(parts, tile, offsets=None):
    stats = [part[pl.ds(CHUNK, STATS), :].astype(jnp.float32) for part in parts]
    tops = [s[4 * tile : 4 * tile + 1] for s in stats]
    totals = [s[4 * tile + 1 : 4 * tile + 2] + s[4 * tile + 2 : 4 * tile + 3] for s in stats]
    best = functools.reduce(jnp.maximum, tops)
    factors = [jnp.exp2(t - best) for t in tops]
    whole = functools.reduce(jnp.add, [t * f for t, f in zip(totals, factors)])
    return factors, best, whole


def columns(rows):
    block = jnp.concatenate(rows + [jnp.zeros((128 - len(rows), 128), jnp.float32)], axis=0)
    turned = jnp.transpose(block)
    return [turned[:, i : i + 1] for i in range(len(rows))]


def merge_into(parts, out_ref):
    stats = []
    for tile in range(TILES):
        factors, best, whole = merge_tile(parts, tile)
        rows = pl.ds(tile * 128, 128)
        terms = [p[rows, :].astype(jnp.float32) * f for p, f in zip(parts, columns(factors))]
        out_ref[rows, :] = functools.reduce(jnp.add, terms).astype(jnp.bfloat16)
        high = near(whole)
        stats += [best, high, whole - high, jnp.zeros_like(best)]
    stats.append(jnp.zeros((STATS - 4 * TILES, 128), jnp.float32))
    out_ref[pl.ds(CHUNK, STATS), :] = jnp.concatenate(stats, axis=0).astype(jnp.bfloat16)


def core_kernel(mine_ref, other_ref, *out_refs):
    for dy in range(Y):
        merge_into([mine_ref.at[dy], other_ref.at[dy]], out_refs[dy])


def y_kernel(*refs):
    merge_into(refs[:Y], refs[Y])


def z_kernel(z_ref, *refs):
    parts, out_ref, spread, merged = refs[:Z], refs[Z], refs[Z + 1], refs[Z + 2]
    z = z_ref[0]
    for k, part in enumerate(parts):
        block = [part[pl.ds(CHUNK, STATS), :].astype(jnp.float32)]
        block.append(jnp.zeros((128 - STATS, 128), jnp.float32))
        turned = jnp.transpose(jnp.concatenate(block, axis=0))
        for tile in range(TILES):
            rows = pl.ds(tile * 128, 128)
            c = turned[:, 4 * tile : 4 * tile + 1]
            t = turned[:, 4 * tile + 1 : 4 * tile + 2] + turned[:, 4 * tile + 2 : 4 * tile + 3]
            spread[0, k, rows, :] = jnp.broadcast_to(c, (128, 128))
            spread[1, k, rows, :] = jnp.broadcast_to(t, (128, 128))
    for place in range(Z):
        sums, tops, totals = [], [], []
        for k, part in enumerate(parts):
            rows = pl.ds(pl.multiple_of((z ^ place ^ k) * ROWS, 32), ROWS)
            sums.append(part[rows, :].astype(jnp.float32))
            tops.append(spread[0, k, rows, :])
            totals.append(spread[1, k, rows, :])
        best = functools.reduce(jnp.maximum, tops)
        factors = [jnp.exp2(t - best) for t in tops]
        out = functools.reduce(jnp.add, [s * f for s, f in zip(sums, factors)])
        whole = functools.reduce(jnp.add, [t * f for t, f in zip(totals, factors)])
        merged[pl.ds(place * ROWS, ROWS), :] = out / whole
    for head in range(HEADS_LOCAL):
        rows = merged[pl.ds(head, Z * LOCAL, stride=HEADS_LOCAL), :]
        out_ref[:, head * WIDTH : (head + 1) * WIDTH] = rows.astype(jnp.bfloat16)


def project_kernel(place_ref, mine_ref, other_ref, weight_ref, out_ref, terms):
    weight = weight_ref[...]
    for dc, ref in enumerate((mine_ref, other_ref)):
        for dy in range(Y):
            terms[dc * Y + dy] = jnp.dot(ref[dy], weight, preferred_element_type=jnp.float32)
    y, c = place_ref[1], place_ref[2]
    for there_y in range(Y):
        for there_c in range(C):
            found = terms[(c ^ there_c) * Y + (y ^ there_y)]
            for z in range(Z):
                row = ((z * Y + there_y) * C + there_c) * LOCAL
                out_ref[row : row + LOCAL, :] = found[z * LOCAL : (z + 1) * LOCAL]


VMEM = pl.BlockSpec(memory_space=pltpu.VMEM)
SMEM = pl.BlockSpec(memory_space=pltpu.SMEM)


def per_device(
    queries,
    prompt_keys,
    prompt_values,
    suffix_keys,
    suffix_values,
    suffix_lengths,
    slot_of_sample,
    out_weight,
):
    me = lax.axis_index("seq")
    z, y, c = me // (Y * C), me // C % Y, me % C
    place = jnp.stack([z, y, c]).astype(jnp.int32)
    bf16 = jnp.bfloat16

    mine = queries.reshape(ROWS, WIDTH)
    by_z = jnp.concatenate([mine] + [exchange(mine, d, 0, 0) for d in range(1, Z)])
    by_y = jnp.concatenate([by_z] + [exchange(by_z, 0, d, 0) for d in range(1, Y)])
    every = jnp.concatenate([by_y, exchange(by_y, 0, 0, 1)])

    slots = me * LOCAL + jnp.arange(LOCAL, dtype=jnp.int32)
    matches = (slot_of_sample[None, :] == slots[:, None]).astype(jnp.int32)
    samples = jnp.sum(matches * jnp.arange(SEQ * LOCAL, dtype=jnp.int32)[None, :], axis=1)
    away = (samples // LOCAL) ^ me
    spot = (away % C) * (Y * Z) + (away // C % Y) * Z + away // (Y * C)
    rows = spot * ROWS + samples % LOCAL * HEADS_LOCAL

    half = jax.ShapeDtypeStruct((Y, PART, WIDTH), bf16)
    part = jax.ShapeDtypeStruct((PART, WIDTH), bf16)
    total_rows = SEQ * ROWS
    prompt = prompt_keys.shape[0]
    first, second = pl.pallas_call(
        attention_kernel,
        out_shape=(half, half),
        in_specs=[SMEM, SMEM, VMEM, VMEM, VMEM] + [pl.BlockSpec(memory_space=pl.ANY)] * 2,
        out_specs=(VMEM, VMEM),
        scratch_shapes=[
            pltpu.VMEM((LOCAL, SUFFIX, WIDTH), bf16),
            pltpu.VMEM((LOCAL, SUFFIX, WIDTH), bf16),
            pltpu.VMEM((prompt, 2 * WIDTH), bf16),
            pltpu.VMEM((2, BLOCK, prompt), jnp.float32),
            pltpu.VMEM((total_rows, WIDTH), jnp.float32),
            pltpu.VMEM((total_rows, WIDTH), jnp.float32),
            pltpu.VMEM((total_rows, WIDTH), jnp.float32),
            pltpu.SemaphoreType.DMA((2,)),
        ],
        compiler_params=pltpu.CompilerParams(vmem_limit_bytes=48 * 2**20),
        name="attention",
    )(
        rows.astype(jnp.int32),
        suffix_lengths,
        every,
        prompt_keys.reshape(prompt, WIDTH),
        prompt_values.reshape(prompt, WIDTH),
        suffix_keys.reshape(LOCAL, SUFFIX, WIDTH),
        suffix_values.reshape(LOCAL, SUFFIX, WIDTH),
    )

    arrived = exchange(second, 0, 0, 1)
    by_dy = pl.pallas_call(
        core_kernel,
        out_shape=(part,) * Y,
        in_specs=[VMEM] * 2,
        out_specs=(VMEM,) * Y,
        name="merge_core",
    )(first, arrived)
    merged = pl.pallas_call(
        y_kernel, out_shape=part, in_specs=[VMEM] * Y, out_specs=VMEM, name="merge_y"
    )(by_dy[0], *[exchange(by_dy[d], 0, d, 0) for d in range(1, Y)])
    attention = pl.pallas_call(
        z_kernel,
        out_shape=jax.ShapeDtypeStruct((Z * LOCAL, HEADS_LOCAL * WIDTH), bf16),
        in_specs=[SMEM] + [VMEM] * Z,
        out_specs=VMEM,
        scratch_shapes=[
            pltpu.VMEM((2, Z, CHUNK, 128), jnp.float32),
            pltpu.VMEM((CHUNK, 128), jnp.float32),
        ],
        name="merge_z",
    )(place, merged, *[exchange(merged, d, 0, 0) for d in range(1, Z)])

    ours = jnp.stack([attention] + [exchange(attention, 0, d, 0) for d in range(1, Y)])
    theirs = exchange(ours, 0, 0, 1)
    depth, columns_local = out_weight.shape
    terms = pl.pallas_call(
        project_kernel,
        out_shape=jax.ShapeDtypeStruct((SEQ * LOCAL, columns_local), jnp.float32),
        in_specs=[SMEM] + [VMEM] * 3,
        out_specs=VMEM,
        scratch_shapes=[pltpu.VMEM((C * Y, Z * LOCAL, columns_local), jnp.float32)],
        name="project",
    )(place, ours, theirs, out_weight)
    heads = lax.axis_size("head")
    terms = terms.astype(bf16).reshape(heads, SEQ * LOCAL // heads, columns_local)
    swapped = lax.all_to_all(terms, "head", split_axis=0, concat_axis=0, tiled=True)
    return jnp.sum(swapped.astype(jnp.float32), axis=0)


def solution(mesh):
    placed = (
        P("seq", "head", None),
        P("seq", "head", None),
        P("seq", "head", None),
        P("seq", "head", None, None),
        P("seq", "head", None, None),
        P("seq"),
        P(),
        P("head", "seq"),
    )
    return jax.shard_map(
        per_device, mesh=mesh, in_specs=placed, out_specs=P("head", "seq"), check_vma=False
    )
```

```python
import functools
import math

import jax
import jax.numpy as jnp
from jax import lax
from jax.experimental import pallas as pl
from jax.experimental.pallas import tpu as pltpu
from jax.sharding import PartitionSpec as P

Z, Y, C = 4, 4, 2
SEQ = Z * Y * C
HEADS_LOCAL = 8
WIDTH = 128
LOCAL = 12
ROWS = LOCAL * HEADS_LOCAL
CHUNK = Z * ROWS
STATS = 16
PART = CHUNK + STATS
TILES = CHUNK // 128
SUFFIX = 1024
BLOCK = 256
EXPONENT = math.log2(math.e) / math.sqrt(WIDTH)
DEAD = -1e30
AROUND_Z = (0, 1, 3, 2)
AROUND_Y = (2, 1, 3)


def exchange(x, dz, dy, dc):
    def index(z, y, c):
        return (z * Y + y) * C + c

    pairs = [
        (index(z, y, c), index(z ^ dz, y ^ dy, c ^ dc))
        for z in range(Z)
        for y in range(Y)
        for c in range(C)
    ]
    return lax.ppermute(x, "seq", pairs)


def join_kernel(*refs):
    for i, ref in enumerate(refs[:-1]):
        refs[-1][i] = ref[...]


def join_z_kernel(info_ref, *refs):
    z = info_ref[2 * LOCAL]
    for offset, ref in zip(AROUND_Z, refs[:-1]):
        refs[-1][z ^ offset] = ref[...]


def join(kernel, pieces, *scalars):
    return pl.pallas_call(
        kernel,
        out_shape=jax.ShapeDtypeStruct((len(pieces), *pieces[0].shape), pieces[0].dtype),
        in_specs=[SMEM] * len(scalars) + [VMEM] * len(pieces),
        out_specs=VMEM,
        compiler_params=PARAMS,
        name="join",
    )(*scalars, *pieces)


def gather_y(x):
    found = {d: exchange(x, 0, d, 0) for d in AROUND_Y}
    return join(join_kernel, [x] + [found[d] for d in range(1, Y)])


def copy_kernel(in_ref, out_ref):
    out_ref[...] = in_ref[...]


def near(x):
    return x.astype(jnp.bfloat16).astype(jnp.float32)


def attention_kernel(
    info_ref,
    mine_ref,
    other_ref,
    keys_hbm,
    values_hbm,
    tail_keys_hbm,
    tail_values_hbm,
    first_ref,
    second_ref,
    queries_ref,
    keys_ref,
    wide_ref,
    tail_k,
    tail_v,
    scores,
    acc,
    total,
    top,
    sem,
):
    pairs = [
        (keys_hbm, keys_ref),
        (values_hbm, wide_ref.at[:, pl.ds(0, WIDTH)]),
        (tail_keys_hbm, tail_k),
        (tail_values_hbm, tail_v),
    ]
    copies = [pltpu.make_async_copy(a, b, sem.at[i]) for i, (a, b) in enumerate(pairs)]
    for copy in copies:
        copy.start()
    wide_ref[:, WIDTH:] = jnp.ones_like(wide_ref[:, WIDTH:])
    queries_ref[: Y * CHUNK] = mine_ref[...]
    queries_ref[Y * CHUNK :] = other_ref[...]
    nt = (((1,), (1,)), ((), ()))

    def score(block, slot):
        q = queries_ref[pl.ds(block * BLOCK, BLOCK), :]
        scores[slot] = lax.dot_general(q, keys_ref[...], nt, preferred_element_type=jnp.float32)

    def weigh(block, slot):
        s = scores[slot]
        c = near(jnp.max(s, axis=1, keepdims=True) * EXPONENT)
        w = jnp.exp2(s * EXPONENT - c).astype(jnp.bfloat16)
        o = jnp.dot(w, wide_ref[...], preferred_element_type=jnp.float32)
        rows = pl.ds(block * BLOCK, BLOCK)
        acc[rows, :] = o[:, :WIDTH]
        total[rows, :] = o[:, WIDTH:]
        top[rows, :] = jnp.broadcast_to(c, (BLOCK, WIDTH))

    blocks = SEQ * ROWS // BLOCK
    copies[0].wait()
    score(0, 0)
    copies[1].wait()
    for i in range(blocks):
        if i + 1 < blocks:
            score(i + 1, (i + 1) % 2)
        weigh(i, i % 2)

    copies[2].wait()
    copies[3].wait()
    position = lax.broadcasted_iota(jnp.int32, (HEADS_LOCAL, SUFFIX), 1)
    tails = []
    for j in range(LOCAL):
        row = info_ref[j]
        base = pl.multiple_of(row // 16 * 16, 16)
        pair = queries_ref[pl.ds(base, 16), :].astype(jnp.float32)
        q = jnp.where(row % 16 == 8, pair[8:], pair[:8]).astype(jnp.bfloat16)
        s = lax.dot_general(q, tail_k[j], nt, preferred_element_type=jnp.float32)
        tails.append(jnp.where(position < info_ref[LOCAL + j], s * EXPONENT, DEAD))
    for j in range(LOCAL):
        c = near(jnp.max(tails[j], axis=1, keepdims=True))
        w = jnp.exp2(tails[j] - c)
        t = jnp.sum(w, axis=1, keepdims=True)
        o = jnp.dot(w.astype(jnp.bfloat16), tail_v[j], preferred_element_type=jnp.float32)
        rows = pl.ds(pl.multiple_of(info_ref[j], 8), 8)
        old = top[rows, :]
        new = jnp.maximum(old, c)
        f, g = jnp.exp2(old - new), jnp.exp2(c - new)
        acc[rows, :] = acc[rows, :] * f + o * g
        total[rows, :] = total[rows, :] * f + t * g
        top[rows, :] = new

    lane = lax.broadcasted_iota(jnp.int32, (128, 128), 1)
    for chunk in range(C * Y):
        part = (first_ref if chunk < Y else second_ref).at[chunk % Y]
        stats = []
        for tile in range(TILES):
            rows = pl.ds(chunk * CHUNK + tile * 128, 128)
            part[pl.ds(tile * 128, 128), :] = acc[rows, :].astype(part.dtype)
            sums = total[rows, :]
            high = near(sums)
            mixed = jnp.where(lane == 0, top[rows, :], jnp.where(lane == 1, high, sums - high))
            stats.append(jnp.transpose(mixed)[:4])
        stats.append(jnp.zeros((STATS - 4 * TILES, 128), jnp.float32))
        part[pl.ds(CHUNK, STATS), :] = jnp.concatenate(stats, axis=0).astype(part.dtype)


def columns(rows):
    block = jnp.concatenate(rows + [jnp.zeros((128 - len(rows), 128), jnp.float32)], axis=0)
    turned = jnp.transpose(block)
    return [turned[:, i : i + 1] for i in range(len(rows))]


def merge_tile(parts, tile):
    stats = [part[pl.ds(CHUNK, STATS), :].astype(jnp.float32) for part in parts]
    tops = [s[4 * tile : 4 * tile + 1] for s in stats]
    totals = [s[4 * tile + 1 : 4 * tile + 2] + s[4 * tile + 2 : 4 * tile + 3] for s in stats]
    best = functools.reduce(jnp.maximum, tops)
    factors = [jnp.exp2(t - best) for t in tops]
    total = functools.reduce(jnp.add, [t * f for t, f in zip(totals, factors)])
    return factors, best, total


def weighted(parts, tile, factors):
    rows = pl.ds(tile * 128, 128)
    terms = [p[rows, :].astype(jnp.float32) * f for p, f in zip(parts, columns(factors))]
    return functools.reduce(jnp.add, terms)


def merge_into(parts, out_refs):
    stats = []
    for tile in range(TILES):
        factors, best, total = merge_tile(parts, tile)
        out = weighted(parts, tile, factors)
        for ref in out_refs:
            ref[pl.ds(tile * 128, 128), :] = out.astype(ref.dtype)
        high = near(total)
        stats += [best, high, total - high, jnp.zeros_like(best)]
    stats.append(jnp.zeros((STATS - 4 * TILES, 128), jnp.float32))
    for ref in out_refs:
        ref[pl.ds(CHUNK, STATS), :] = jnp.concatenate(stats, axis=0).astype(ref.dtype)


def core_kernel(mine_ref, other_ref, *out_refs):
    for dy in range(Y):
        merge_into([mine_ref.at[dy], other_ref.at[dy]], [out_refs[dy]])


def merge_kernel(*refs):
    merge_into(refs[:-2], refs[-2:])


def finish_kernel(mine_ref, other_ref, out_ref, merged):
    parts = [mine_ref, other_ref]
    for tile in range(TILES):
        factors, _, total = merge_tile(parts, tile)
        merged[pl.ds(tile * 128, 128), :] = weighted(parts, tile, [f / total for f in factors])
    for head in range(HEADS_LOCAL):
        rows = merged[pl.ds(head, Z * LOCAL, stride=HEADS_LOCAL), :]
        out_ref[:, head * WIDTH : (head + 1) * WIDTH] = rows.astype(out_ref.dtype)


def project_kernel(info_ref, mine_ref, other_ref, weight_ref, out_ref, terms):
    weight = weight_ref[...]
    for dc, ref in enumerate((mine_ref, other_ref)):
        for dy in range(Y):
            terms[dc * Y + dy] = lax.dot_general(
                ref[dy], weight, (((1,), (1,)), ((), ())), preferred_element_type=jnp.float32
            )
    y, c = info_ref[2 * LOCAL + 1], info_ref[2 * LOCAL + 2]
    for there_y in range(Y):
        for there_c in range(C):
            found = terms[(c ^ there_c) * Y + (y ^ there_y)]
            for z in range(Z):
                row = ((z * Y + there_y) * C + there_c) * LOCAL
                out_ref[row : row + LOCAL, :] = found[z * LOCAL : (z + 1) * LOCAL].astype(out_ref.dtype)


VMEM = pl.BlockSpec(memory_space=pltpu.VMEM)
SMEM = pl.BlockSpec(memory_space=pltpu.SMEM)
PARAMS = pltpu.CompilerParams(vmem_limit_bytes=32 * 2**20)


def per_device(
    queries,
    prompt_keys,
    prompt_values,
    suffix_keys,
    suffix_values,
    suffix_lengths,
    slot_of_sample,
    out_weight,
):
    me = lax.axis_index("seq")
    z, y, c = me // (Y * C), me // C % Y, me % C
    bf16 = jnp.bfloat16

    slots = me * LOCAL + jnp.arange(LOCAL, dtype=jnp.int32)
    matches = (slot_of_sample[None, :] == slots[:, None]).astype(jnp.int32)
    samples = jnp.sum(matches * jnp.arange(SEQ * LOCAL, dtype=jnp.int32)[None, :], axis=1)
    away = (samples // LOCAL) ^ me
    spot = (away % C) * (Y * Z) + (away // C % Y) * Z + samples // (LOCAL * Y * C)
    rows = spot * ROWS + samples % LOCAL * HEADS_LOCAL
    place = jnp.stack([z, y, c])
    info = jnp.concatenate([rows, suffix_lengths, place]).astype(jnp.int32)

    def shape(dtype, *more):
        return jax.ShapeDtypeStruct((*more, PART, WIDTH), dtype)

    total_rows = SEQ * ROWS
    prompt = prompt_keys.shape[0]
    caches = [
        pltpu.with_memory_space_constraint(x, pltpu.HBM)
        for x in (
            prompt_keys.reshape(prompt, WIDTH),
            prompt_values.reshape(prompt, WIDTH),
            suffix_keys.reshape(LOCAL, SUFFIX, WIDTH),
            suffix_values.reshape(LOCAL, SUFFIX, WIDTH),
        )
    ]
    mine = queries.reshape(ROWS, WIDTH)
    found = [exchange(mine, d, 0, 0) for d in AROUND_Z[1:]]
    held = pl.pallas_call(
        copy_kernel,
        out_shape=jax.ShapeDtypeStruct(mine.shape, bf16),
        in_specs=[VMEM],
        out_specs=VMEM,
        compiler_params=PARAMS,
        name="hold",
    )(mine)
    by_z = join(join_z_kernel, [held] + found, info).reshape(CHUNK, WIDTH)
    by_y = gather_y(by_z).reshape(Y * CHUNK, WIDTH)
    first, second = pl.pallas_call(
        attention_kernel,
        out_shape=(shape(jnp.float32, Y), shape(bf16, Y)),
        in_specs=[SMEM] + [VMEM] * 2 + [pl.BlockSpec(memory_space=pltpu.HBM)] * 4,
        out_specs=(VMEM, VMEM),
        scratch_shapes=[
            pltpu.VMEM((total_rows, WIDTH), bf16),
            pltpu.VMEM((prompt, WIDTH), bf16),
            pltpu.VMEM((prompt, 2 * WIDTH), bf16),
            pltpu.VMEM((LOCAL, SUFFIX, WIDTH), bf16),
            pltpu.VMEM((LOCAL, SUFFIX, WIDTH), bf16),
            pltpu.VMEM((2, BLOCK, prompt), jnp.float32),
            pltpu.VMEM((total_rows, WIDTH), jnp.float32),
            pltpu.VMEM((total_rows, WIDTH), jnp.float32),
            pltpu.VMEM((total_rows, WIDTH), jnp.float32),
            pltpu.SemaphoreType.DMA((4,)),
        ],
        compiler_params=PARAMS,
        name="attention",
    )(info, by_y, exchange(by_y, 0, 0, 1), *caches)

    arrived = exchange(second, 0, 0, 1)
    by_dy = pl.pallas_call(
        core_kernel,
        out_shape=(shape(jnp.float32),) + (shape(bf16),) * (Y - 1),
        in_specs=[VMEM] * 2,
        out_specs=(VMEM,) * Y,
        compiler_params=PARAMS,
        name="merge_core",
    )(first, arrived)

    def merge(name, *parts):
        return pl.pallas_call(
            merge_kernel,
            out_shape=(shape(jnp.float32), shape(bf16)),
            in_specs=[VMEM] * len(parts),
            out_specs=(VMEM,) * 2,
            compiler_params=PARAMS,
            name=name,
        )(*parts)

    kept, sent = merge("merge_y", by_dy[0], *[exchange(by_dy[d], 0, d, 0) for d in AROUND_Y])
    kept, sent = merge("merge_z", kept, exchange(sent, 1, 0, 0))
    attention = pl.pallas_call(
        finish_kernel,
        out_shape=jax.ShapeDtypeStruct((Z * LOCAL, HEADS_LOCAL * WIDTH), bf16),
        in_specs=[VMEM] * 2,
        out_specs=VMEM,
        scratch_shapes=[pltpu.VMEM((CHUNK, WIDTH), jnp.float32)],
        compiler_params=PARAMS,
        name="finish",
    )(kept, exchange(sent, 3, 0, 0))

    ours = gather_y(attention)
    theirs = exchange(ours, 0, 0, 1)
    columns_local = out_weight.shape[1]
    terms = pl.pallas_call(
        project_kernel,
        out_shape=jax.ShapeDtypeStruct((SEQ * LOCAL, columns_local), bf16),
        in_specs=[SMEM] + [VMEM] * 3,
        out_specs=VMEM,
        scratch_shapes=[pltpu.VMEM((C * Y, Z * LOCAL, columns_local), jnp.float32)],
        compiler_params=PARAMS,
        name="project",
    )(info, ours, theirs, out_weight.T)
    heads = lax.axis_size("head")
    terms = terms.reshape(heads, SEQ * LOCAL // heads, columns_local)
    swapped = lax.all_to_all(terms, "head", split_axis=0, concat_axis=0, tiled=True)
    return jnp.sum(swapped.astype(jnp.float32), axis=0)


def solution(mesh):
    placed = (
        P("seq", "head", None),
        P("seq", "head", None),
        P("seq", "head", None),
        P("seq", "head", None, None),
        P("seq", "head", None, None),
        P("seq"),
        P(),
        P("head", "seq"),
    )
    return jax.shard_map(
        per_device, mesh=mesh, in_specs=placed, out_specs=P("head", "seq"), check_vma=False
    )
```

```python
import functools
import math

import jax
import jax.numpy as jnp
from jax import lax
from jax.experimental import pallas as pl
from jax.experimental.pallas import tpu as pltpu
from jax.sharding import PartitionSpec as P

Z, Y, C = 4, 4, 2
SEQ = Z * Y * C
HEADS_LOCAL = 8
WIDTH = 128
LOCAL = 12
ROWS = LOCAL * HEADS_LOCAL
CHUNK = Z * ROWS
STATS = 16
PART = CHUNK + STATS
TILES = CHUNK // 128
SUFFIX = 1024
BLOCK = 384
EXPONENT = math.log2(math.e) / math.sqrt(WIDTH)
DEAD = -1e30
GROUP = 4
AROUND_Z = (0, 1, 3, 2)
AROUND_Y = (2, 1, 3)


def exchange(x, dz, dy, dc):
    def index(z, y, c):
        return (z * Y + y) * C + c

    pairs = [
        (index(z, y, c), index(z ^ dz, y ^ dy, c ^ dc))
        for z in range(Z)
        for y in range(Y)
        for c in range(C)
    ]
    return lax.ppermute(x, "seq", pairs)


def join_kernel(*refs):
    for i, ref in enumerate(refs[:-1]):
        refs[-1][i] = ref[...]


def join_z_kernel(*refs):
    z = lax.axis_index("seq") // (Y * C)
    for offset, ref in zip(AROUND_Z, refs[:-1]):
        refs[-1][z ^ offset] = ref[...]


def join(kernel, pieces):
    return pl.pallas_call(
        kernel,
        out_shape=jax.ShapeDtypeStruct((len(pieces), *pieces[0].shape), pieces[0].dtype),
        in_specs=[VMEM] * len(pieces),
        out_specs=VMEM,
        compiler_params=PARAMS,
        name="join",
    )(*pieces)


def gather_y(x):
    found = {d: exchange(x, 0, d, 0) for d in AROUND_Y}
    return join(join_kernel, [x] + [found[d] for d in range(1, Y)])


def copy_kernel(in_ref, out_ref):
    out_ref[...] = in_ref[...]


def near(x):
    return x.astype(jnp.bfloat16).astype(jnp.float32)


def attend(half, info_in, queries_ref, keys_ref, wide_ref, tail_k, tail_v, part_ref, scores, acc, total, top, chosen, info_ref, sem):
    copy = pltpu.make_async_copy(info_in, info_ref, sem.at[0])
    copy.start()
    nt = (((1,), (1,)), ((), ()))
    rows_here = Y * CHUNK

    def score(block, slot):
        q = queries_ref[pl.ds(block * BLOCK, BLOCK), :]
        scores[slot] = lax.dot_general(q, keys_ref[...], nt, preferred_element_type=jnp.float32)

    def weigh(block, slot):
        s = scores[slot]
        c = near(jnp.max(s, axis=1, keepdims=True) * EXPONENT)
        w = jnp.exp2(s * EXPONENT - c).astype(jnp.bfloat16)
        o = jnp.dot(w, wide_ref[...], preferred_element_type=jnp.float32)
        rows = pl.ds(block * BLOCK, BLOCK)
        acc[rows, :] = o[:, :WIDTH]
        total[rows, :] = o[:, WIDTH:]
        top[rows, :] = jnp.broadcast_to(c, (BLOCK, WIDTH))

    blocks = rows_here // BLOCK
    score(0, 0)
    for i in range(blocks):
        if i + 1 < blocks:
            score(i + 1, (i + 1) % 2)
        weigh(i, i % 2)

    copy.wait()
    spare = pl.ds(rows_here, HEADS_LOCAL)
    for ref in (acc, total, top):
        ref[spare, :] = jnp.zeros((HEADS_LOCAL, WIDTH), jnp.float32)
    for k in range(LOCAL + 1):
        chosen[k] = 0
    count = jnp.int32(0)
    for j in range(LOCAL):
        chosen[count] = j
        count = count + (info_ref[j] // rows_here == half).astype(jnp.int32)
    position = lax.broadcasted_iota(jnp.int32, (HEADS_LOCAL, SUFFIX), 1)

    def group(start):
        spots, tails, slots = [], [], []
        for k in range(start, start + GROUP):
            j = chosen[k]
            spot = jnp.where(k < count, info_ref[j] - half * rows_here, rows_here)
            row = jnp.where(k < count, spot, 0)
            base = pl.multiple_of(row // 16 * 16, 16)
            pair = queries_ref[pl.ds(base, 16), :].astype(jnp.float32)
            q = jnp.where(row % 16 == 8, pair[8:], pair[:8]).astype(jnp.bfloat16)
            s = lax.dot_general(q, tail_k[j], nt, preferred_element_type=jnp.float32)
            tails.append(jnp.where(position < info_ref[LOCAL + j], s * EXPONENT, DEAD))
            spots.append(spot)
            slots.append(j)
        parts = []
        for j, s in zip(slots, tails):
            c = near(jnp.max(s, axis=1, keepdims=True))
            w = jnp.exp2(s - c)
            t = jnp.sum(w, axis=1, keepdims=True)
            o = jnp.dot(w.astype(jnp.bfloat16), tail_v[j], preferred_element_type=jnp.float32)
            parts.append((c, t, o))
        for spot, (c, t, o) in zip(spots, parts):
            rows = pl.ds(pl.multiple_of(spot, 8), HEADS_LOCAL)
            old = top[rows, :]
            new = jnp.maximum(old, c)
            f, g = jnp.exp2(old - new), jnp.exp2(c - new)
            acc[rows, :] = acc[rows, :] * f + o * g
            total[rows, :] = total[rows, :] * f + t * g
            top[rows, :] = new

    for start in range(0, LOCAL, GROUP):
        pl.when(start < count)(functools.partial(group, start))

    lane = lax.broadcasted_iota(jnp.int32, (128, 128), 1)
    for chunk in range(Y):
        part = part_ref.at[chunk]
        stats = []
        for tile in range(TILES):
            rows = pl.ds(chunk * CHUNK + tile * 128, 128)
            part[pl.ds(tile * 128, 128), :] = acc[rows, :].astype(part.dtype)
            sums = total[rows, :]
            high = near(sums)
            mixed = jnp.where(lane == 0, top[rows, :], jnp.where(lane == 1, high, sums - high))
            stats.append(jnp.transpose(mixed)[:4])
        stats.append(jnp.zeros((STATS - 4 * TILES, 128), jnp.float32))
        part[pl.ds(CHUNK, STATS), :] = jnp.concatenate(stats, axis=0).astype(part.dtype)


def prepare_kernel(after_ref, keys_hbm, values_hbm, tail_keys_hbm, tail_values_hbm, keys_ref, wide_ref, tail_k, tail_v, sem):
    pairs = [
        (keys_hbm, keys_ref),
        (values_hbm, wide_ref.at[:, pl.ds(0, WIDTH)]),
        (tail_keys_hbm, tail_k),
        (tail_values_hbm, tail_v),
    ]
    copies = [pltpu.make_async_copy(a, b, sem.at[i]) for i, (a, b) in enumerate(pairs)]
    for copy in copies:
        copy.start()
    wide_ref[:, WIDTH:] = jnp.ones_like(wide_ref[:, WIDTH:])
    for copy in copies:
        copy.wait()


def columns(rows):
    block = jnp.concatenate(rows + [jnp.zeros((128 - len(rows), 128), jnp.float32)], axis=0)
    turned = jnp.transpose(block)
    return [turned[:, i : i + 1] for i in range(len(rows))]


def merge_tile(parts, tile):
    stats = [part[pl.ds(CHUNK, STATS), :].astype(jnp.float32) for part in parts]
    tops = [s[4 * tile : 4 * tile + 1] for s in stats]
    totals = [s[4 * tile + 1 : 4 * tile + 2] + s[4 * tile + 2 : 4 * tile + 3] for s in stats]
    best = functools.reduce(jnp.maximum, tops)
    factors = [jnp.exp2(t - best) for t in tops]
    total = functools.reduce(jnp.add, [t * f for t, f in zip(totals, factors)])
    return factors, best, total


def weighted(parts, tile, factors):
    rows = pl.ds(tile * 128, 128)
    terms = [p[rows, :].astype(jnp.float32) * f for p, f in zip(parts, columns(factors))]
    return functools.reduce(jnp.add, terms)


def merge_into(parts, out_refs):
    stats = []
    for tile in range(TILES):
        factors, best, total = merge_tile(parts, tile)
        out = weighted(parts, tile, factors)
        for ref in out_refs:
            ref[pl.ds(tile * 128, 128), :] = out.astype(ref.dtype)
        high = near(total)
        stats += [best, high, total - high, jnp.zeros_like(best)]
    stats.append(jnp.zeros((STATS - 4 * TILES, 128), jnp.float32))
    for ref in out_refs:
        ref[pl.ds(CHUNK, STATS), :] = jnp.concatenate(stats, axis=0).astype(ref.dtype)


def core_kernel(mine_ref, other_ref, *out_refs):
    for dy in range(Y):
        merge_into([mine_ref.at[dy], other_ref.at[dy]], [out_refs[dy]])


def merge_kernel(*refs):
    merge_into(refs[:-2], refs[-2:])


def finish_kernel(mine_ref, other_ref, out_ref, merged):
    parts = [mine_ref, other_ref]
    for tile in range(TILES):
        factors, _, total = merge_tile(parts, tile)
        merged[pl.ds(tile * 128, 128), :] = weighted(parts, tile, [f / total for f in factors])
    for head in range(HEADS_LOCAL):
        rows = merged[pl.ds(head, Z * LOCAL, stride=HEADS_LOCAL), :]
        out_ref[:, head * WIDTH : (head + 1) * WIDTH] = rows.astype(out_ref.dtype)


def project_kernel(mine_ref, other_ref, weight_ref, out_ref, terms):
    weight = weight_ref[...]
    for dc, ref in enumerate((mine_ref, other_ref)):
        for dy in range(Y):
            terms[dc * Y + dy] = lax.dot_general(
                ref[dy], weight, (((1,), (1,)), ((), ())), preferred_element_type=jnp.float32
            )
    me = lax.axis_index("seq")
    y, c = me // C % Y, me % C
    for there_y in range(Y):
        for there_c in range(C):
            found = terms[(c ^ there_c) * Y + (y ^ there_y)]
            for z in range(Z):
                row = ((z * Y + there_y) * C + there_c) * LOCAL
                out_ref[row : row + LOCAL, :] = found[z * LOCAL : (z + 1) * LOCAL].astype(out_ref.dtype)


VMEM = pl.BlockSpec(memory_space=pltpu.VMEM)
SMEM = pl.BlockSpec(memory_space=pltpu.SMEM)
PARAMS = pltpu.CompilerParams(vmem_limit_bytes=32 * 2**20)


def per_device(
    queries,
    prompt_keys,
    prompt_values,
    suffix_keys,
    suffix_values,
    suffix_lengths,
    slot_of_sample,
    out_weight,
):
    me = lax.axis_index("seq")
    bf16 = jnp.bfloat16

    slots = me * LOCAL + jnp.arange(LOCAL, dtype=jnp.int32)
    matches = (slot_of_sample[None, :] == slots[:, None]).astype(jnp.int32)
    samples = jnp.sum(matches * jnp.arange(SEQ * LOCAL, dtype=jnp.int32)[None, :], axis=1)
    away = (samples // LOCAL) ^ me
    spot = (away % C) * (Y * Z) + (away // C % Y) * Z + samples // (LOCAL * Y * C)
    rows = spot * ROWS + samples % LOCAL * HEADS_LOCAL
    info = jnp.concatenate([rows, suffix_lengths]).astype(jnp.int32)

    def shape(dtype, *more):
        return jax.ShapeDtypeStruct((*more, PART, WIDTH), dtype)

    prompt = prompt_keys.shape[0]
    caches = [
        pltpu.with_memory_space_constraint(x, pltpu.HBM)
        for x in (
            prompt_keys.reshape(prompt, WIDTH),
            prompt_values.reshape(prompt, WIDTH),
            suffix_keys.reshape(LOCAL, SUFFIX, WIDTH),
            suffix_values.reshape(LOCAL, SUFFIX, WIDTH),
        )
    ]
    mine = queries.reshape(ROWS, WIDTH)
    found = [exchange(mine, d, 0, 0) for d in AROUND_Z[1:]]
    held = pl.pallas_call(
        copy_kernel,
        out_shape=jax.ShapeDtypeStruct(mine.shape, bf16),
        in_specs=[VMEM],
        out_specs=VMEM,
        compiler_params=PARAMS,
        name="hold",
    )(mine)
    by_z = join(join_z_kernel, [held] + found).reshape(CHUNK, WIDTH)
    by_y = gather_y(by_z).reshape(Y * CHUNK, WIDTH)
    half_rows = Y * CHUNK
    scratch = [pltpu.VMEM((2, BLOCK, prompt), jnp.float32)]
    scratch += [pltpu.VMEM((half_rows + HEADS_LOCAL, WIDTH), jnp.float32)] * 3
    scratch += [pltpu.SMEM((LOCAL + 4,), jnp.int32), pltpu.SMEM((2 * LOCAL,), jnp.int32)]
    scratch += [pltpu.SemaphoreType.DMA((1,))]
    cost = pl.CostEstimate(
        flops=4 * half_rows * prompt * WIDTH, bytes_accessed=2**23, transcendentals=half_rows * prompt
    )
    tail = jax.ShapeDtypeStruct((LOCAL, SUFFIX, WIDTH), bf16)
    by_core = exchange(by_y, 0, 0, 1)
    held = pl.pallas_call(
        prepare_kernel,
        out_shape=(
            jax.ShapeDtypeStruct((prompt, WIDTH), bf16),
            jax.ShapeDtypeStruct((prompt, 2 * WIDTH), bf16),
            tail,
            tail,
        ),
        in_specs=[VMEM] + [pl.BlockSpec(memory_space=pltpu.HBM)] * 4,
        out_specs=(VMEM,) * 4,
        scratch_shapes=[pltpu.SemaphoreType.DMA((4,))],
        compiler_params=PARAMS,
        cost_estimate=pl.CostEstimate(flops=0, bytes_accessed=2**23, transcendentals=0),
        name="prepare",
    )(by_z, *caches)

    def attend_to(half, queries, dtype):
        return pl.pallas_call(
            functools.partial(attend, half),
            out_shape=shape(dtype, Y),
            in_specs=[pl.BlockSpec(memory_space=pl.ANY)] + [VMEM] * 5,
            out_specs=VMEM,
            scratch_shapes=scratch,
            compiler_params=PARAMS,
            cost_estimate=cost,
            name=f"attention_{half}",
        )(info, queries, *held)

    arrived = exchange(attend_to(0, by_y, bf16), 0, 0, 1)
    second = attend_to(1, by_core, jnp.float32)
    by_dy = pl.pallas_call(
        core_kernel,
        out_shape=(shape(jnp.float32),) + (shape(bf16),) * (Y - 1),
        in_specs=[VMEM] * 2,
        out_specs=(VMEM,) * Y,
        compiler_params=PARAMS,
        name="merge_core",
    )(second, arrived)

    def merge(name, *parts):
        return pl.pallas_call(
            merge_kernel,
            out_shape=(shape(jnp.float32), shape(bf16)),
            in_specs=[VMEM] * len(parts),
            out_specs=(VMEM,) * 2,
            compiler_params=PARAMS,
            name=name,
        )(*parts)

    kept, sent = merge("merge_y", by_dy[0], *[exchange(by_dy[d], 0, d, 0) for d in AROUND_Y])
    kept, sent = merge("merge_z", kept, exchange(sent, 1, 0, 0))
    attention = pl.pallas_call(
        finish_kernel,
        out_shape=jax.ShapeDtypeStruct((Z * LOCAL, HEADS_LOCAL * WIDTH), bf16),
        in_specs=[VMEM] * 2,
        out_specs=VMEM,
        scratch_shapes=[pltpu.VMEM((CHUNK, WIDTH), jnp.float32)],
        compiler_params=PARAMS,
        name="finish",
    )(kept, exchange(sent, 3, 0, 0))

    ours = gather_y(attention)
    theirs = exchange(ours, 0, 0, 1)
    columns_local = out_weight.shape[1]
    terms = pl.pallas_call(
        project_kernel,
        out_shape=jax.ShapeDtypeStruct((SEQ * LOCAL, columns_local), bf16),
        in_specs=[VMEM] * 3,
        out_specs=VMEM,
        scratch_shapes=[pltpu.VMEM((C * Y, Z * LOCAL, columns_local), jnp.float32)],
        compiler_params=PARAMS,
        name="project",
    )(theirs, ours, out_weight.T)
    heads = lax.axis_size("head")
    terms = terms.reshape(heads, SEQ * LOCAL // heads, columns_local)
    swapped = lax.all_to_all(terms, "head", split_axis=0, concat_axis=0, tiled=True)
    return jnp.sum(swapped.astype(jnp.float32), axis=0)


def solution(mesh):
    placed = (
        P("seq", "head", None),
        P("seq", "head", None),
        P("seq", "head", None),
        P("seq", "head", None, None),
        P("seq", "head", None, None),
        P("seq"),
        P(),
        P("head", "seq"),
    )
    return jax.shard_map(
        per_device, mesh=mesh, in_specs=placed, out_specs=P("head", "seq"), check_vma=False
    )
```

```python
import functools
import math

import jax
import jax.numpy as jnp
from jax import lax
from jax.experimental import pallas as pl
from jax.experimental.pallas import tpu as pltpu
from jax.sharding import PartitionSpec as P

Z, Y, C = 4, 4, 2
SEQ = Z * Y * C
HEADS_LOCAL = 8
WIDTH = 128
LOCAL = 12
ROWS = LOCAL * HEADS_LOCAL
CHUNK = Z * ROWS
STATS = 16
PART = CHUNK + STATS
TILES = CHUNK // 128
SUFFIX = 1024
EXPONENT = math.log2(math.e) / math.sqrt(WIDTH)
DEAD = -1e30
NT = (((1,), (1,)), ((), ()))
GROUP = 4
AROUND_Z = (0, 1, 3, 2)
AROUND_Y = (2, 1, 3)


def exchange(x, dz, dy, dc):
    def index(z, y, c):
        return (z * Y + y) * C + c

    pairs = [
        (index(z, y, c), index(z ^ dz, y ^ dy, c ^ dc))
        for z in range(Z)
        for y in range(Y)
        for c in range(C)
    ]
    return lax.ppermute(x, "seq", pairs)


def join_kernel(*refs):
    for i, ref in enumerate(refs[:-1]):
        refs[-1][i] = ref[...]


def join_z_kernel(*refs):
    z = lax.axis_index("seq") // (Y * C)
    for offset, ref in zip(AROUND_Z, refs[:-1]):
        refs[-1][z ^ offset] = ref[...]


def join(kernel, pieces):
    return pl.pallas_call(
        kernel,
        out_shape=jax.ShapeDtypeStruct((len(pieces), *pieces[0].shape), pieces[0].dtype),
        in_specs=[VMEM] * len(pieces),
        out_specs=VMEM,
        compiler_params=PARAMS,
        name="join",
    )(*pieces)


def gather_y(x):
    found = {d: exchange(x, 0, d, 0) for d in AROUND_Y}
    return join(join_kernel, [x] + [found[d] for d in range(1, Y)])


def copy_kernel(in_ref, out_ref):
    out_ref[...] = in_ref[...]


def near(x):
    return x.astype(jnp.bfloat16).astype(jnp.float32)


def prefix(queries_ref, places, keys_ref, wide_ref, scores, put):
    def score(i):
        q = queries_ref[pl.ds(places[i], CHUNK), :]
        scores[i % 2] = lax.dot_general(q, keys_ref[...], NT, preferred_element_type=jnp.float32)

    score(0)
    for i in range(len(places)):
        if i + 1 < len(places):
            score(i + 1)
        s = scores[i % 2]
        c = near(jnp.max(s, axis=1, keepdims=True) * EXPONENT)
        w = jnp.exp2(s * EXPONENT - c).astype(jnp.bfloat16)
        o = jnp.dot(w, wide_ref[...], preferred_element_type=jnp.float32)
        put(i, (o[:, :WIDTH], o[:, WIDTH:], jnp.broadcast_to(c, (CHUNK, WIDTH))))


def emit(part_ref, acc, total, top, start):
    lane = lax.broadcasted_iota(jnp.int32, (128, 128), 1)
    stats = []
    for tile in range(TILES):
        rows = pl.ds(start + tile * 128, 128)
        part_ref[pl.ds(tile * 128, 128), :] = acc[rows, :].astype(part_ref.dtype)
        sums = total[rows, :]
        high = near(sums)
        mixed = jnp.where(lane == 0, top[rows, :], jnp.where(lane == 1, high, sums - high))
        stats.append(jnp.transpose(mixed)[:4])
    stats.append(jnp.zeros((STATS - 4 * TILES, 128), jnp.float32))
    part_ref[pl.ds(CHUNK, STATS), :] = jnp.concatenate(stats, axis=0).astype(part_ref.dtype)


def add_suffixes(half, queries_ref, tail_k, tail_v, state, chosen, info_ref):
    acc, total, top = state
    rows_here = Y * CHUNK
    for ref in state:
        ref[pl.ds(rows_here, HEADS_LOCAL), :] = jnp.zeros((HEADS_LOCAL, WIDTH), jnp.float32)
    for k in range(LOCAL + 1):
        chosen[k] = 0
    count = jnp.int32(0)
    for j in range(LOCAL):
        chosen[count] = j
        count = count + (info_ref[j] // rows_here == half).astype(jnp.int32)
    position = lax.broadcasted_iota(jnp.int32, (HEADS_LOCAL, SUFFIX), 1)

    def group(start):
        spots, tails, slots = [], [], []
        for k in range(start, start + GROUP):
            j = chosen[k]
            spot = jnp.where(k < count, info_ref[j] - half * rows_here, rows_here)
            row = jnp.where(k < count, spot, 0)
            base = pl.multiple_of(row // 16 * 16, 16)
            pair = queries_ref[pl.ds(base, 16), :].astype(jnp.float32)
            q = jnp.where(row % 16 == 8, pair[8:], pair[:8]).astype(jnp.bfloat16)
            s = lax.dot_general(q, tail_k[j], NT, preferred_element_type=jnp.float32)
            tails.append(jnp.where(position < info_ref[LOCAL + j], s * EXPONENT, DEAD))
            spots.append(spot)
            slots.append(j)
        parts = []
        for j, s in zip(slots, tails):
            c = near(jnp.max(s, axis=1, keepdims=True))
            w = jnp.exp2(s - c)
            t = jnp.sum(w, axis=1, keepdims=True)
            o = jnp.dot(w.astype(jnp.bfloat16), tail_v[j], preferred_element_type=jnp.float32)
            parts.append((c, t, o))
        for spot, (c, t, o) in zip(spots, parts):
            rows = pl.ds(pl.multiple_of(spot, 8), HEADS_LOCAL)
            old = top[rows, :]
            new = jnp.maximum(old, c)
            f, g = jnp.exp2(old - new), jnp.exp2(c - new)
            acc[rows, :] = acc[rows, :] * f + o * g
            total[rows, :] = total[rows, :] * f + t * g
            top[rows, :] = new

    for start in range(0, LOCAL, GROUP):
        pl.when(start < count)(functools.partial(group, start))


def own_kernel(queries_ref, keys_ref, wide_ref, acc, total, top, scores):
    def put(_, found):
        for ref, value in zip((acc, total, top), found):
            ref[...] = value

    prefix(queries_ref, [0], keys_ref, wide_ref, scores, put)


def first_kernel(info_in, queries_ref, keys_ref, wide_ref, tail_k, tail_v, *refs):
    begun, part_ref, scores, state, (chosen, info_ref, sem) = refs[:3], refs[3], refs[4], refs[5:8], refs[8:]
    copy = pltpu.make_async_copy(info_in, info_ref, sem.at[0])
    copy.start()
    for ref, old in zip(state, begun):
        ref[:CHUNK, :] = old[...]
    places = [CHUNK, 2 * CHUNK, 3 * CHUNK]

    def put(i, found):
        for ref, value in zip(state, found):
            ref[pl.ds(places[i], CHUNK), :] = value

    prefix(queries_ref, places, keys_ref, wide_ref, scores, put)
    copy.wait()
    add_suffixes(0, queries_ref, tail_k, tail_v, state, chosen, info_ref)
    for dy in range(Y):
        emit(part_ref.at[dy], *state, dy * CHUNK)


def second_kernel(info_in, queries_ref, keys_ref, wide_ref, tail_k, tail_v, part_ref, scores, *refs):
    state, (chosen, info_ref, sem) = refs[:3], refs[3:]
    copy = pltpu.make_async_copy(info_in, info_ref, sem.at[0])
    copy.start()
    places = [dy * CHUNK for dy in range(Y)]

    def put(i, found):
        for ref, value in zip(state, found):
            ref[pl.ds(places[i], CHUNK), :] = value

    prefix(queries_ref, places, keys_ref, wide_ref, scores, put)
    copy.wait()
    add_suffixes(1, queries_ref, tail_k, tail_v, state, chosen, info_ref)
    for dy in range(Y):
        emit(part_ref.at[dy], *state, dy * CHUNK)


def prepare_kernel(keys_hbm, values_hbm, keys_ref, wide_ref, sem):
    copies = [
        pltpu.make_async_copy(keys_hbm, keys_ref, sem.at[0]),
        pltpu.make_async_copy(values_hbm, wide_ref.at[:, pl.ds(0, WIDTH)], sem.at[1]),
    ]
    for copy in copies:
        copy.start()
    wide_ref[:, WIDTH:] = jnp.ones_like(wide_ref[:, WIDTH:])
    for copy in copies:
        copy.wait()


def fetch_kernel(after_ref, tail_keys_hbm, tail_values_hbm, tail_k, tail_v, sem):
    copies = [
        pltpu.make_async_copy(tail_keys_hbm, tail_k, sem.at[0]),
        pltpu.make_async_copy(tail_values_hbm, tail_v, sem.at[1]),
    ]
    for copy in copies:
        copy.start()
    for copy in copies:
        copy.wait()


def columns(rows):
    block = jnp.concatenate(rows + [jnp.zeros((128 - len(rows), 128), jnp.float32)], axis=0)
    turned = jnp.transpose(block)
    return [turned[:, i : i + 1] for i in range(len(rows))]


def merge_tile(parts, tile):
    stats = [part[pl.ds(CHUNK, STATS), :].astype(jnp.float32) for part in parts]
    tops = [s[4 * tile : 4 * tile + 1] for s in stats]
    totals = [s[4 * tile + 1 : 4 * tile + 2] + s[4 * tile + 2 : 4 * tile + 3] for s in stats]
    best = functools.reduce(jnp.maximum, tops)
    factors = [jnp.exp2(t - best) for t in tops]
    total = functools.reduce(jnp.add, [t * f for t, f in zip(totals, factors)])
    return factors, best, total


def weighted(parts, tile, factors):
    rows = pl.ds(tile * 128, 128)
    terms = [p[rows, :].astype(jnp.float32) * f for p, f in zip(parts, columns(factors))]
    return functools.reduce(jnp.add, terms)


def merge_into(parts, out_refs):
    stats = []
    for tile in range(TILES):
        factors, best, total = merge_tile(parts, tile)
        out = weighted(parts, tile, factors)
        for ref in out_refs:
            ref[pl.ds(tile * 128, 128), :] = out.astype(ref.dtype)
        high = near(total)
        stats += [best, high, total - high, jnp.zeros_like(best)]
    stats.append(jnp.zeros((STATS - 4 * TILES, 128), jnp.float32))
    for ref in out_refs:
        ref[pl.ds(CHUNK, STATS), :] = jnp.concatenate(stats, axis=0).astype(ref.dtype)


def core_kernel(mine_ref, other_ref, *out_refs):
    for dy in range(Y):
        merge_into([mine_ref.at[dy], other_ref.at[dy]], [out_refs[dy]])


def merge_kernel(*refs):
    merge_into(refs[:-2], refs[-2:])


def finish_kernel(mine_ref, other_ref, out_ref, merged):
    parts = [mine_ref, other_ref]
    for tile in range(TILES):
        factors, _, total = merge_tile(parts, tile)
        merged[pl.ds(tile * 128, 128), :] = weighted(parts, tile, [f / total for f in factors])
    for head in range(HEADS_LOCAL):
        rows = merged[pl.ds(head, Z * LOCAL, stride=HEADS_LOCAL), :]
        out_ref[:, head * WIDTH : (head + 1) * WIDTH] = rows.astype(out_ref.dtype)


def project_kernel(mine_ref, other_ref, weight_ref, out_ref, terms):
    weight = weight_ref[...]
    for dc, ref in enumerate((mine_ref, other_ref)):
        for dy in range(Y):
            terms[dc * Y + dy] = lax.dot_general(
                ref[dy], weight, (((1,), (1,)), ((), ())), preferred_element_type=jnp.float32
            )
    me = lax.axis_index("seq")
    y, c = me // C % Y, me % C
    for there_y in range(Y):
        for there_c in range(C):
            found = terms[(c ^ there_c) * Y + (y ^ there_y)]
            for z in range(Z):
                row = ((z * Y + there_y) * C + there_c) * LOCAL
                out_ref[row : row + LOCAL, :] = found[z * LOCAL : (z + 1) * LOCAL].astype(out_ref.dtype)


VMEM = pl.BlockSpec(memory_space=pltpu.VMEM)
SMEM = pl.BlockSpec(memory_space=pltpu.SMEM)
PARAMS = pltpu.CompilerParams(vmem_limit_bytes=32 * 2**20)


def per_device(
    queries,
    prompt_keys,
    prompt_values,
    suffix_keys,
    suffix_values,
    suffix_lengths,
    slot_of_sample,
    out_weight,
):
    me = lax.axis_index("seq")
    bf16 = jnp.bfloat16

    slots = me * LOCAL + jnp.arange(LOCAL, dtype=jnp.int32)
    matches = (slot_of_sample[None, :] == slots[:, None]).astype(jnp.int32)
    samples = jnp.sum(matches * jnp.arange(SEQ * LOCAL, dtype=jnp.int32)[None, :], axis=1)
    away = (samples // LOCAL) ^ me
    spot = (away % C) * (Y * Z) + (away // C % Y) * Z + samples // (LOCAL * Y * C)
    rows = spot * ROWS + samples % LOCAL * HEADS_LOCAL
    info = jnp.concatenate([rows, suffix_lengths]).astype(jnp.int32)

    def shape(dtype, *more):
        return jax.ShapeDtypeStruct((*more, PART, WIDTH), dtype)

    prompt = prompt_keys.shape[0]
    caches = [
        pltpu.with_memory_space_constraint(x, pltpu.HBM)
        for x in (
            prompt_keys.reshape(prompt, WIDTH),
            prompt_values.reshape(prompt, WIDTH),
            suffix_keys.reshape(LOCAL, SUFFIX, WIDTH),
            suffix_values.reshape(LOCAL, SUFFIX, WIDTH),
        )
    ]
    mine = queries.reshape(ROWS, WIDTH)
    found = [exchange(mine, d, 0, 0) for d in AROUND_Z[1:]]
    held = pl.pallas_call(
        copy_kernel,
        out_shape=jax.ShapeDtypeStruct(mine.shape, bf16),
        in_specs=[VMEM],
        out_specs=VMEM,
        compiler_params=PARAMS,
        name="hold",
    )(mine)
    by_z = join(join_z_kernel, [held] + found).reshape(CHUNK, WIDTH)
    by_y = gather_y(by_z).reshape(Y * CHUNK, WIDTH)
    def call(kernel, name, out, ins, *operands, scratch=(), chunks=0):
        return pl.pallas_call(
            kernel,
            out_shape=out,
            in_specs=ins + [VMEM] * (len(operands) - len(ins)),
            out_specs=jax.tree.map(lambda _: VMEM, out),
            scratch_shapes=list(scratch),
            compiler_params=PARAMS,
            cost_estimate=pl.CostEstimate(
                flops=4 * chunks * CHUNK * prompt * WIDTH,
                bytes_accessed=2**22,
                transcendentals=chunks * CHUNK * prompt,
            ),
            name=name,
        )(*operands)

    anywhere = [pl.BlockSpec(memory_space=pl.ANY)]
    hbm = pl.BlockSpec(memory_space=pltpu.HBM)
    two = [pltpu.SemaphoreType.DMA((2,))]
    scores = [pltpu.VMEM((2, CHUNK, prompt), jnp.float32)]
    state = [pltpu.VMEM((Y * CHUNK + HEADS_LOCAL, WIDTH), jnp.float32)] * 3
    lists = [pltpu.SMEM((LOCAL + 4,), jnp.int32), pltpu.SMEM((2 * LOCAL,), jnp.int32)]
    lists += [pltpu.SemaphoreType.DMA((1,))]
    rows_of = [jax.ShapeDtypeStruct((CHUNK, WIDTH), jnp.float32)] * 3
    tail = jax.ShapeDtypeStruct((LOCAL, SUFFIX, WIDTH), bf16)
    prompt_shapes = [
        jax.ShapeDtypeStruct((prompt, WIDTH), bf16),
        jax.ShapeDtypeStruct((prompt, 2 * WIDTH), bf16),
    ]
    keys, wide = call(prepare_kernel, "prepare", prompt_shapes, [hbm] * 2, *caches[:2], scratch=two)
    begun = call(own_kernel, "attention_own", rows_of, [], by_z, keys, wide, scratch=scores, chunks=1)
    tails = call(fetch_kernel, "fetch", [tail, tail], [VMEM, hbm, hbm], begun[0], *caches[2:], scratch=two)

    by_core = exchange(by_y, 0, 0, 1)
    first = call(
        first_kernel, "attention_first", shape(bf16, Y), anywhere, info, by_y, keys, wide, *tails, *begun,
        scratch=scores + state + lists, chunks=3,
    )
    arrived = exchange(first, 0, 0, 1)
    second = call(
        second_kernel, "attention_second", shape(jnp.float32, Y), anywhere,
        info, by_core, keys, wide, *tails, scratch=scores + state + lists, chunks=4,
    )
    by_dy = call(
        core_kernel, "merge_core", [shape(jnp.float32)] + [shape(bf16)] * (Y - 1), [], second, arrived
    )

    def merge(name, *parts):
        return pl.pallas_call(
            merge_kernel,
            out_shape=(shape(jnp.float32), shape(bf16)),
            in_specs=[VMEM] * len(parts),
            out_specs=(VMEM,) * 2,
            compiler_params=PARAMS,
            name=name,
        )(*parts)

    kept, sent = merge("merge_y", by_dy[0], *[exchange(by_dy[d], 0, d, 0) for d in AROUND_Y])
    kept, sent = merge("merge_z", kept, exchange(sent, 1, 0, 0))
    attention = pl.pallas_call(
        finish_kernel,
        out_shape=jax.ShapeDtypeStruct((Z * LOCAL, HEADS_LOCAL * WIDTH), bf16),
        in_specs=[VMEM] * 2,
        out_specs=VMEM,
        scratch_shapes=[pltpu.VMEM((CHUNK, WIDTH), jnp.float32)],
        compiler_params=PARAMS,
        name="finish",
    )(kept, exchange(sent, 3, 0, 0))

    ours = gather_y(attention)
    theirs = exchange(ours, 0, 0, 1)
    columns_local = out_weight.shape[1]
    terms = pl.pallas_call(
        project_kernel,
        out_shape=jax.ShapeDtypeStruct((SEQ * LOCAL, columns_local), bf16),
        in_specs=[VMEM] * 3,
        out_specs=VMEM,
        scratch_shapes=[pltpu.VMEM((C * Y, Z * LOCAL, columns_local), jnp.float32)],
        compiler_params=PARAMS,
        name="project",
    )(theirs, ours, out_weight.T)
    heads = lax.axis_size("head")
    terms = terms.reshape(heads, SEQ * LOCAL // heads, columns_local)
    swapped = lax.all_to_all(terms, "head", split_axis=0, concat_axis=0, tiled=True)
    return jnp.sum(swapped.astype(jnp.float32), axis=0)


def solution(mesh):
    placed = (
        P("seq", "head", None),
        P("seq", "head", None),
        P("seq", "head", None),
        P("seq", "head", None, None),
        P("seq", "head", None, None),
        P("seq"),
        P(),
        P("head", "seq"),
    )
    return jax.shard_map(
        per_device, mesh=mesh, in_specs=placed, out_specs=P("head", "seq"), check_vma=False
    )
```

```python
import functools
import math

import jax
import jax.numpy as jnp
from jax import lax
from jax.experimental import pallas as pl
from jax.experimental.pallas import tpu as pltpu
from jax.sharding import PartitionSpec as P

Z, Y, C = 4, 4, 2
SEQ = Z * Y * C
HEADS_LOCAL = 8
WIDTH = 128
LOCAL = 12
ROWS = LOCAL * HEADS_LOCAL
CHUNK = Z * ROWS
STATS = 16
PART = CHUNK + STATS
TILES = CHUNK // 128
SUFFIX = 1024
EXPONENT = math.log2(math.e) / math.sqrt(WIDTH)
DEAD = -1e30
NT = (((1,), (1,)), ((), ()))
GROUP = 4
AROUND_Z = (0, 1, 3, 2)
AROUND_Y = (2, 1, 3)


def exchange(x, dz, dy, dc):
    def index(z, y, c):
        return (z * Y + y) * C + c

    pairs = [
        (index(z, y, c), index(z ^ dz, y ^ dy, c ^ dc))
        for z in range(Z)
        for y in range(Y)
        for c in range(C)
    ]
    return lax.ppermute(x, "seq", pairs)


def join_kernel(*refs):
    for i, ref in enumerate(refs[:-1]):
        refs[-1][i] = ref[...]


def join_z_kernel(*refs):
    z = lax.axis_index("seq") // (Y * C)
    for offset, ref in zip(AROUND_Z, refs[:-1]):
        refs[-1][z ^ offset] = ref[...]


def join(kernel, pieces):
    return pl.pallas_call(
        kernel,
        out_shape=jax.ShapeDtypeStruct((len(pieces), *pieces[0].shape), pieces[0].dtype),
        in_specs=[VMEM] * len(pieces),
        out_specs=VMEM,
        compiler_params=PARAMS,
        name="join",
    )(*pieces)


def around_y(x):
    found = {d: exchange(x, 0, d, 0) for d in AROUND_Y}
    return [x] + [found[d] for d in range(1, Y)]


def copy_kernel(in_ref, out_ref):
    out_ref[...] = in_ref[...]


def near(x):
    return x.astype(jnp.bfloat16).astype(jnp.float32)


def prefix(queries_ref, places, keys_ref, wide_ref, scores, put):
    def score(i):
        q = queries_ref[pl.ds(places[i], CHUNK), :]
        scores[i % 2] = lax.dot_general(q, keys_ref[...], NT, preferred_element_type=jnp.float32)

    score(0)
    for i in range(len(places)):
        if i + 1 < len(places):
            score(i + 1)
        s = scores[i % 2]
        c = near(jnp.max(s, axis=1, keepdims=True) * EXPONENT)
        w = jnp.exp2(s * EXPONENT - c).astype(jnp.bfloat16)
        o = jnp.dot(w, wide_ref[...], preferred_element_type=jnp.float32)
        put(i, (o[:, :WIDTH], o[:, WIDTH:], jnp.broadcast_to(c, (CHUNK, WIDTH))))


def emit(part_ref, acc, total, top, start):
    lane = lax.broadcasted_iota(jnp.int32, (128, 128), 1)
    stats = []
    for tile in range(TILES):
        rows = pl.ds(start + tile * 128, 128)
        part_ref[pl.ds(tile * 128, 128), :] = acc[rows, :].astype(part_ref.dtype)
        sums = total[rows, :]
        high = near(sums)
        mixed = jnp.where(lane == 0, top[rows, :], jnp.where(lane == 1, high, sums - high))
        stats.append(jnp.transpose(mixed)[:4])
    stats.append(jnp.zeros((STATS - 4 * TILES, 128), jnp.float32))
    part_ref[pl.ds(CHUNK, STATS), :] = jnp.concatenate(stats, axis=0).astype(part_ref.dtype)


def add_suffixes(half, queries_ref, tail_k, tail_v, state, chosen, info_ref):
    acc, total, top = state
    rows_here = Y * CHUNK
    for ref in state:
        ref[pl.ds(rows_here, HEADS_LOCAL), :] = jnp.zeros((HEADS_LOCAL, WIDTH), jnp.float32)
    for k in range(LOCAL + 1):
        chosen[k] = 0
    count = jnp.int32(0)
    for j in range(LOCAL):
        chosen[count] = j
        count = count + (info_ref[j] // rows_here == half).astype(jnp.int32)
    position = lax.broadcasted_iota(jnp.int32, (HEADS_LOCAL, SUFFIX), 1)

    def group(start):
        spots, tails, slots = [], [], []
        for k in range(start, start + GROUP):
            j = chosen[k]
            spot = jnp.where(k < count, info_ref[j] - half * rows_here, rows_here)
            row = jnp.where(k < count, spot, 0)
            base = pl.multiple_of(row // 16 * 16, 16)
            pair = queries_ref[pl.ds(base, 16), :].astype(jnp.float32)
            q = jnp.where(row % 16 == 8, pair[8:], pair[:8]).astype(jnp.bfloat16)
            s = lax.dot_general(q, tail_k[j], NT, preferred_element_type=jnp.float32)
            tails.append(jnp.where(position < info_ref[LOCAL + j], s * EXPONENT, DEAD))
            spots.append(spot)
            slots.append(j)
        parts = []
        for j, s in zip(slots, tails):
            c = near(jnp.max(s, axis=1, keepdims=True))
            w = jnp.exp2(s - c)
            t = jnp.sum(w, axis=1, keepdims=True)
            o = jnp.dot(w.astype(jnp.bfloat16), tail_v[j], preferred_element_type=jnp.float32)
            parts.append((c, t, o))
        for spot, (c, t, o) in zip(spots, parts):
            rows = pl.ds(pl.multiple_of(spot, 8), HEADS_LOCAL)
            old = top[rows, :]
            new = jnp.maximum(old, c)
            f, g = jnp.exp2(old - new), jnp.exp2(c - new)
            acc[rows, :] = acc[rows, :] * f + o * g
            total[rows, :] = total[rows, :] * f + t * g
            top[rows, :] = new

    for start in range(0, LOCAL, GROUP):
        pl.when(start < count)(functools.partial(group, start))


def own_kernel(queries_ref, keys_ref, wide_ref, acc, total, top, scores):
    def put(_, found):
        for ref, value in zip((acc, total, top), found):
            ref[...] = value

    prefix(queries_ref, [0], keys_ref, wide_ref, scores, put)


def first_kernel(info_in, queries_ref, keys_ref, wide_ref, tail_keys_hbm, tail_values_hbm, *refs):
    begun, (part_ref, tail_k, tail_v, scores), state, (chosen, info_ref, sem) = refs[:3], refs[3:7], refs[7:10], refs[10:]
    copies = [
        pltpu.make_async_copy(info_in, info_ref, sem.at[0]),
        pltpu.make_async_copy(tail_keys_hbm, tail_k, sem.at[1]),
        pltpu.make_async_copy(tail_values_hbm, tail_v, sem.at[2]),
    ]
    for copy in copies:
        copy.start()
    for ref, old in zip(state, begun):
        ref[:CHUNK, :] = old[...]
    places = [CHUNK, 2 * CHUNK, 3 * CHUNK]

    def put(i, found):
        for ref, value in zip(state, found):
            ref[pl.ds(places[i], CHUNK), :] = value

    prefix(queries_ref, places, keys_ref, wide_ref, scores, put)
    for copy in copies:
        copy.wait()
    add_suffixes(0, queries_ref, tail_k, tail_v, state, chosen, info_ref)
    for dy in range(Y):
        emit(part_ref.at[dy], *state, dy * CHUNK)


def second_kernel(info_in, queries_ref, keys_ref, wide_ref, tail_k, tail_v, part_ref, scores, *refs):
    state, (chosen, info_ref, sem) = refs[:3], refs[3:]
    copy = pltpu.make_async_copy(info_in, info_ref, sem.at[0])
    copy.start()
    places = [dy * CHUNK for dy in range(Y)]

    def put(i, found):
        for ref, value in zip(state, found):
            ref[pl.ds(places[i], CHUNK), :] = value

    prefix(queries_ref, places, keys_ref, wide_ref, scores, put)
    copy.wait()
    add_suffixes(1, queries_ref, tail_k, tail_v, state, chosen, info_ref)
    for dy in range(Y):
        emit(part_ref.at[dy], *state, dy * CHUNK)


def prepare_kernel(keys_hbm, values_hbm, keys_ref, wide_ref, sem):
    copies = [
        pltpu.make_async_copy(keys_hbm, keys_ref, sem.at[0]),
        pltpu.make_async_copy(values_hbm, wide_ref.at[:, pl.ds(0, WIDTH)], sem.at[1]),
    ]
    for copy in copies:
        copy.start()
    wide_ref[:, WIDTH:] = jnp.ones_like(wide_ref[:, WIDTH:])
    for copy in copies:
        copy.wait()


def columns(rows):
    block = jnp.concatenate(rows + [jnp.zeros((128 - len(rows), 128), jnp.float32)], axis=0)
    turned = jnp.transpose(block)
    return [turned[:, i : i + 1] for i in range(len(rows))]


def merge_tile(parts, tile):
    stats = [part[pl.ds(CHUNK, STATS), :].astype(jnp.float32) for part in parts]
    tops = [s[4 * tile : 4 * tile + 1] for s in stats]
    totals = [s[4 * tile + 1 : 4 * tile + 2] + s[4 * tile + 2 : 4 * tile + 3] for s in stats]
    best = functools.reduce(jnp.maximum, tops)
    factors = [jnp.exp2(t - best) for t in tops]
    total = functools.reduce(jnp.add, [t * f for t, f in zip(totals, factors)])
    return factors, best, total


def weighted(parts, tile, factors):
    rows = pl.ds(tile * 128, 128)
    terms = [p[rows, :].astype(jnp.float32) * f for p, f in zip(parts, columns(factors))]
    return functools.reduce(jnp.add, terms)


def merge_into(parts, out_refs):
    stats = []
    for tile in range(TILES):
        factors, best, total = merge_tile(parts, tile)
        out = weighted(parts, tile, factors)
        for ref in out_refs:
            ref[pl.ds(tile * 128, 128), :] = out.astype(ref.dtype)
        high = near(total)
        stats += [best, high, total - high, jnp.zeros_like(best)]
    stats.append(jnp.zeros((STATS - 4 * TILES, 128), jnp.float32))
    for ref in out_refs:
        ref[pl.ds(CHUNK, STATS), :] = jnp.concatenate(stats, axis=0).astype(ref.dtype)


def core_kernel(mine_ref, other_ref, *out_refs):
    for dy in range(Y):
        merge_into([mine_ref.at[dy], other_ref.at[dy]], [out_refs[dy]])


def merge_kernel(*refs):
    merge_into(refs[:-2], refs[-2:])


def finish_kernel(mine_ref, other_ref, out_ref, merged):
    parts = [mine_ref, other_ref]
    for tile in range(TILES):
        factors, _, total = merge_tile(parts, tile)
        merged[pl.ds(tile * 128, 128), :] = weighted(parts, tile, [f / total for f in factors])
    for head in range(HEADS_LOCAL):
        rows = merged[pl.ds(head, Z * LOCAL, stride=HEADS_LOCAL), :]
        out_ref[:, head * WIDTH : (head + 1) * WIDTH] = rows.astype(out_ref.dtype)


def project_kernel(mine_ref, other_ref, weight_ref, out_ref, terms):
    weight = weight_ref[...]
    for dc, ref in enumerate((mine_ref, other_ref)):
        for dy in range(Y):
            terms[dc * Y + dy] = lax.dot_general(
                ref[dy], weight, (((1,), (1,)), ((), ())), preferred_element_type=jnp.float32
            )
    me = lax.axis_index("seq")
    y, c = me // C % Y, me % C
    for there_y in range(Y):
        for there_c in range(C):
            found = terms[(c ^ there_c) * Y + (y ^ there_y)]
            for z in range(Z):
                row = ((z * Y + there_y) * C + there_c) * LOCAL
                out_ref[row : row + LOCAL, :] = found[z * LOCAL : (z + 1) * LOCAL].astype(out_ref.dtype)


VMEM = pl.BlockSpec(memory_space=pltpu.VMEM)
SMEM = pl.BlockSpec(memory_space=pltpu.SMEM)
PARAMS = pltpu.CompilerParams(vmem_limit_bytes=32 * 2**20)


def per_device(
    queries,
    prompt_keys,
    prompt_values,
    suffix_keys,
    suffix_values,
    suffix_lengths,
    slot_of_sample,
    out_weight,
):
    me = lax.axis_index("seq")
    bf16 = jnp.bfloat16

    slots = me * LOCAL + jnp.arange(LOCAL, dtype=jnp.int32)
    matches = (slot_of_sample[None, :] == slots[:, None]).astype(jnp.int32)
    samples = jnp.sum(matches * jnp.arange(SEQ * LOCAL, dtype=jnp.int32)[None, :], axis=1)
    away = (samples // LOCAL) ^ me
    spot = (away % C) * (Y * Z) + (away // C % Y) * Z + samples // (LOCAL * Y * C)
    rows = spot * ROWS + samples % LOCAL * HEADS_LOCAL
    info = jnp.concatenate([rows, suffix_lengths]).astype(jnp.int32)

    def shape(dtype, *more):
        return jax.ShapeDtypeStruct((*more, PART, WIDTH), dtype)

    prompt = prompt_keys.shape[0]
    caches = [
        pltpu.with_memory_space_constraint(x, pltpu.HBM)
        for x in (
            prompt_keys.reshape(prompt, WIDTH),
            prompt_values.reshape(prompt, WIDTH),
            suffix_keys.reshape(LOCAL, SUFFIX, WIDTH),
            suffix_values.reshape(LOCAL, SUFFIX, WIDTH),
        )
    ]
    def call(kernel, name, out, ins, *operands, scratch=(), chunks=0):
        return pl.pallas_call(
            kernel,
            out_shape=out,
            in_specs=ins + [VMEM] * (len(operands) - len(ins)),
            out_specs=jax.tree.map(lambda _: VMEM, out),
            scratch_shapes=list(scratch),
            compiler_params=PARAMS,
            cost_estimate=pl.CostEstimate(
                flops=4 * chunks * CHUNK * prompt * WIDTH,
                bytes_accessed=2**22,
                transcendentals=chunks * CHUNK * prompt,
            ),
            name=name,
        )(*operands)

    anywhere = [pl.BlockSpec(memory_space=pl.ANY)]
    hbm = pl.BlockSpec(memory_space=pltpu.HBM)
    two = [pltpu.SemaphoreType.DMA((2,))]
    scores = [pltpu.VMEM((2, CHUNK, prompt), jnp.float32)]
    state = [pltpu.VMEM((Y * CHUNK + HEADS_LOCAL, WIDTH), jnp.float32)] * 3
    lists = [pltpu.SMEM((LOCAL + 4,), jnp.int32), pltpu.SMEM((2 * LOCAL,), jnp.int32)]
    lists += [pltpu.SemaphoreType.DMA((3,))]
    rows_of = [jax.ShapeDtypeStruct((CHUNK, WIDTH), jnp.float32)] * 3
    tail = jax.ShapeDtypeStruct((LOCAL, SUFFIX, WIDTH), bf16)
    prompt_shapes = [
        jax.ShapeDtypeStruct((prompt, WIDTH), bf16),
        jax.ShapeDtypeStruct((prompt, 2 * WIDTH), bf16),
    ]
    keys, wide = call(prepare_kernel, "prepare", prompt_shapes, [hbm] * 2, *caches[:2], scratch=two)
    mine = queries.reshape(ROWS, WIDTH)
    found = [exchange(mine, d, 0, 0) for d in AROUND_Z[1:]]
    held = pl.pallas_call(
        copy_kernel,
        out_shape=jax.ShapeDtypeStruct(mine.shape, bf16),
        in_specs=[VMEM],
        out_specs=VMEM,
        compiler_params=PARAMS,
        name="hold",
    )(mine)
    found, keys, wide = lax.optimization_barrier((found, keys, wide))
    by_z = join(join_z_kernel, [held] + found).reshape(CHUNK, WIDTH)
    pieces = around_y(by_z)
    begun = call(own_kernel, "attention_own", rows_of, [], by_z, keys, wide, scratch=scores, chunks=1)

    pieces, begun, info = lax.optimization_barrier((pieces, begun, info))
    by_y = join(join_kernel, pieces).reshape(Y * CHUNK, WIDTH)
    by_core = exchange(by_y, 0, 0, 1)
    first, *tails = call(
        first_kernel, "attention_first", [shape(bf16, Y), tail, tail], anywhere + [VMEM] * 3 + [hbm] * 2,
        info, by_y, keys, wide, *caches[2:], *begun, scratch=scores + state + lists, chunks=3,
    )
    arrived = exchange(first, 0, 0, 1)
    second = call(
        second_kernel, "attention_second", shape(jnp.float32, Y), anywhere,
        info, by_core, keys, wide, *tails, scratch=scores + state + lists, chunks=4,
    )
    by_dy = call(
        core_kernel, "merge_core", [shape(jnp.float32)] + [shape(bf16)] * (Y - 1), [], second, arrived
    )

    def merge(name, *parts):
        return pl.pallas_call(
            merge_kernel,
            out_shape=(shape(jnp.float32), shape(bf16)),
            in_specs=[VMEM] * len(parts),
            out_specs=(VMEM,) * 2,
            compiler_params=PARAMS,
            name=name,
        )(*parts)

    kept, sent = merge("merge_y", by_dy[0], *[exchange(by_dy[d], 0, d, 0) for d in AROUND_Y])
    kept, sent = merge("merge_z", kept, exchange(sent, 1, 0, 0))
    attention = pl.pallas_call(
        finish_kernel,
        out_shape=jax.ShapeDtypeStruct((Z * LOCAL, HEADS_LOCAL * WIDTH), bf16),
        in_specs=[VMEM] * 2,
        out_specs=VMEM,
        scratch_shapes=[pltpu.VMEM((CHUNK, WIDTH), jnp.float32)],
        compiler_params=PARAMS,
        name="finish",
    )(kept, exchange(sent, 3, 0, 0))

    ours = join(join_kernel, around_y(attention))
    theirs = exchange(ours, 0, 0, 1)
    columns_local = out_weight.shape[1]
    terms = pl.pallas_call(
        project_kernel,
        out_shape=jax.ShapeDtypeStruct((SEQ * LOCAL, columns_local), bf16),
        in_specs=[VMEM] * 3,
        out_specs=VMEM,
        scratch_shapes=[pltpu.VMEM((C * Y, Z * LOCAL, columns_local), jnp.float32)],
        compiler_params=PARAMS,
        name="project",
    )(theirs, ours, out_weight.T)
    heads = lax.axis_size("head")
    terms = terms.reshape(heads, SEQ * LOCAL // heads, columns_local)
    swapped = lax.all_to_all(terms, "head", split_axis=0, concat_axis=0, tiled=True)
    return jnp.sum(swapped.astype(jnp.float32), axis=0)


def solution(mesh):
    placed = (
        P("seq", "head", None),
        P("seq", "head", None),
        P("seq", "head", None),
        P("seq", "head", None, None),
        P("seq", "head", None, None),
        P("seq"),
        P(),
        P("head", "seq"),
    )
    return jax.shard_map(
        per_device, mesh=mesh, in_specs=placed, out_specs=P("head", "seq"), check_vma=False
    )
```
